32 devices in a mesh: dp: 4 (over z), wide: 4 (over y, x), narrow: 2 (over core).
Axes of the slice: x: 2, y: 2, z: 4, core: 2. Of those that a mesh axis runs over, the one named last changes fastest.
Arguments:
- tokens: bfloat16 [1024, 4, 1088], P('wide', 'dp', 'narrow'), may hold values from -6 to 6
- segments: int32 [1024, 4], P(None, 'dp'), may hold values from 0 to 7, as said below
- cotangent: bfloat16 [1024, 4, 1088], P('wide', 'dp', 'narrow'), may hold values from -6 to 6
- norm1_gain: float32 [2, 1088], replicated, may hold values from 0.25 to 1.75
- norm1_shift: float32 [2, 1088], replicated, may hold values from -3 to 3
- qkv_weight: bfloat16 [2, 1088, 3264], P(None, 'narrow', 'wide'), may hold values from -0.1875 to 0.1875
- qv_bias: float32 [2, 2, 1088], replicated, may hold values from -3 to 3
- out_weight: bfloat16 [2, 1088, 1088], P(None, 'wide', 'narrow'), may hold values from -0.75 to 0.75
- out_bias: float32 [2, 1088], replicated, may hold values from -3 to 3
- norm2_gain: float32 [2, 1088], replicated, may hold values from 0.25 to 1.75
- norm2_shift: float32 [2, 1088], replicated, may hold values from -3 to 3
- up_weight: bfloat16 [2, 1088, 4352], P(None, 'narrow', 'wide'), may hold values from -0.1875 to 0.1875
- up_bias: float32 [2, 4352], replicated, may hold values from -3 to 3
- down_weight: bfloat16 [2, 4352, 1088], P(None, 'wide', 'narrow'), may hold values from -0.09375 to 0.09375
- down_bias: float32 [2, 1088], replicated, may hold values from -3 to 3
Outputs:
- output: bfloat16 [1024, 4, 1088], P('wide', 'dp', 'narrow')
- input_grad: float32 [1024, 4, 1088], P('wide', 'dp', 'narrow')
- grad_norm1_gain: float32 [2, 1088], replicated
- grad_norm1_shift: float32 [2, 1088], replicated
- grad_qkv_weight: float32 [2, 1088, 3264], P(None, 'narrow', 'wide')
- grad_qv_bias: float32 [2, 2, 1088], replicated
- grad_out_weight: float32 [2, 1088, 1088], P(None, 'wide', 'narrow')
- grad_out_bias: float32 [2, 1088], replicated
- grad_norm2_gain: float32 [2, 1088], replicated
- grad_norm2_shift: float32 [2, 1088], replicated
- grad_up_weight: float32 [2, 1088, 4352], P(None, 'narrow', 'wide')
- grad_up_bias: float32 [2, 4352], replicated
- grad_down_weight: float32 [2, 4352, 1088], P(None, 'wide', 'narrow')
- grad_down_bias: float32 [2, 1088], replicated
The draws below stay inside these ranges and needn't reach their ends.
Inputs may be any that keep to these rules, and one draw needn't show every extreme that they name: `segments`: in every sequence the segment numbers start at 0 and never fall along the positions; equal numbers mark one document.
All inputs are finite; a program needn't handle non-finite values.
Results may differ from the reference program's by a relative error of at most 0.014.
Values may be sent and summed in bfloat16 or wider, within the bound.
A program may use at most 192 MiB of HBM per device.

```python
import jax
import jax.numpy as jnp
from jax import lax

D = 1088
HEADS = 17
HEAD = 64
FF = 4352
LAYERS = 2
LEN = 1024
SEQ_G = 1
SEQS = 4


def draw_segments(key, part):
    key = jax.random.fold_in(key, 11)
    flag_key, pick_key, place_key = jax.random.split(key, 3)
    position = jnp.arange(LEN)[:, None]
    flags = jax.random.randint(flag_key, (LEN, SEQS), 0, LEN)
    chosen = jax.random.randint(pick_key, (SEQS // SEQ_G,), 0, SEQ_G)
    column = jnp.arange(SEQS)
    single = column % SEQ_G == jnp.repeat(chosen, SEQ_G)
    tail = LEN // 8
    edge = (position < tail) | (position >= LEN - tail)
    drawn = flags < 4
    dense = (flags < 16) & edge
    starts = jnp.where(single[None, :], dense, drawn) & (position > 0)
    places = jax.random.permutation(place_key, tail)[:7] + (LEN - tail)
    forced = jnp.zeros((LEN,), jnp.int32).at[places].set(1) > 0
    starts = starts | forced[:, None] & (column == chosen[0])[None, :]
    counts = jnp.cumsum(starts.astype(jnp.int32), axis=0).astype(jnp.int32)
    return jnp.minimum(counts, 7).astype(jnp.int32)


def steps_of(stream_key, dims, cuts, smallest, high):
    gain, own = 1.0, jax.random.fold_in(stream_key, 6)
    for axis_at, shards_of in cuts:
        steps = jnp.exp(jax.random.uniform(jax.random.fold_in(own, axis_at), (shards_of,), jnp.float32, smallest / len(cuts), high / len(cuts)))
        gain = gain * jnp.repeat(steps, dims[axis_at] // shards_of).reshape([-1 if axis == axis_at else 1 for axis in range(len(dims))])
    return gain


def centred(rng, shape, scale, limit, cuts=(), held_as=jnp.bfloat16):
    factor_of = steps_of(rng, shape, cuts, -0.22, 0.18) if cuts else 1.0
    drawn = jax.random.normal(rng, shape, jnp.float32) * scale * factor_of
    return jnp.minimum(jnp.maximum(drawn, -limit), limit).astype(held_as)


def setup_inputs(seed: int = 0) -> dict:
    seeds = jax.random.split(jax.random.key(seed), 16)
    return {
        "tokens": centred(seeds[0], (LEN, SEQS, D), 1.0, 6.0, ((0, 4), (1, 4), (2, 2))),
        "segments": draw_segments(jax.random.fold_in(seeds[15], 71), 0),
        "cotangent": centred(seeds[2], (LEN, SEQS, D), 1.0, 6.0, ((0, 4), (1, 4), (2, 2))),
        "norm1_gain": jnp.clip(1.0 + 0.15 * jax.random.normal(seeds[3], (LAYERS, D), jnp.float32), 0.25, 1.75),
        "norm1_shift": centred(seeds[4], (LAYERS, D), 0.3, 3.0, (), jnp.float32),
        "qkv_weight": centred(seeds[5], (LAYERS, D, 3 * D), D ** -0.5, 0.1875, ((1, 2), (2, 4))),
        "qv_bias": centred(seeds[6], (LAYERS, 2, D), 0.3, 3.0, (), jnp.float32),
        "out_weight": centred(seeds[7], (LAYERS, D, D), (D // 16) ** -0.5, 0.75, ((1, 4), (2, 2))),
        "out_bias": centred(seeds[8], (LAYERS, D), 0.3, 3.0, (), jnp.float32),
        "norm2_gain": jnp.clip(1.0 + 0.15 * jax.random.normal(seeds[9], (LAYERS, D), jnp.float32), 0.25, 1.75),
        "norm2_shift": centred(seeds[10], (LAYERS, D), 0.3, 3.0, (), jnp.float32),
        "up_weight": centred(seeds[11], (LAYERS, D, FF), D ** -0.5, 0.1875, ((1, 2), (2, 4))),
        "up_bias": centred(seeds[12], (LAYERS, FF), 0.3, 3.0, (), jnp.float32),
        "down_weight": centred(seeds[13], (LAYERS, FF, D), FF ** -0.5, 0.09375, ((1, 4), (2, 2))),
        "down_bias": centred(seeds[14], (LAYERS, D), 0.3, 3.0, (), jnp.float32),
    }


HIGHEST = lax.Precision.HIGHEST
EPSILON = 1e-05
NEGATIVE = -1e+30
SCORE_SCALE = 0.125

@jax.custom_vjp
def low(v):
    return lax.optimization_barrier(v.astype(jnp.bfloat16)).astype(jnp.float32)

@jax.custom_vjp
def low_back(v):
    return v

def low_keep(v):
    return (low(v), None)

def low_pass(kept, grad):
    return (grad,)

def back_keep(v):
    return (v, None)

def back_low(kept, grad):
    return (low(grad),)
low.defvjp(low_keep, low_pass)
low_back.defvjp(back_keep, back_low)

def layer_norm(values, gain_vec, shift_vec):
    average = lax.optimization_barrier(jnp.mean(values, -1, keepdims=True))
    centered = values - average
    variance = lax.optimization_barrier(jnp.mean(centered * centered, -1, keepdims=True))
    return centered * lax.rsqrt(variance + EPSILON) * gain_vec + shift_vec

def attend_one(operands):
    queries, key_rows, value_rows, seg_row = operands
    scores = low_back(jnp.einsum('qhe,khe->hqk', queries, key_rows, precision=HIGHEST) * SCORE_SCALE)
    position = jnp.arange(queries.shape[0])
    allowed = (seg_row[None, :] == seg_row[:, None]) & (position[None, :] <= position[:, None])
    weights = jax.nn.softmax(jnp.where(allowed[None], scores, NEGATIVE), axis=-1)
    return jnp.einsum('hqk,khe->qhe', low(weights), value_rows, precision=HIGHEST)

def split_sequences(tensor):
    return jnp.transpose(tensor.reshape(LEN, SEQS, HEADS, HEAD), (1, 0, 2, 3))

def block_layer(residual, segments, tensor_list):
    norm1_gain, norm1_shift, qkv_weight, qv_bias, out_weight, out_bias, norm2_gain, norm2_shift, up_weight, up_bias, down_weight, down_bias = tensor_list
    normed = low(layer_norm(residual, norm1_gain, norm1_shift))
    bias_row = jnp.concatenate([qv_bias[0], jnp.zeros_like(qv_bias[0]), qv_bias[1]])
    projected = jnp.einsum('psd,df->psf', normed, qkv_weight, precision=HIGHEST) + bias_row
    projected = low(low_back(projected))
    queries = split_sequences(projected[:, :, :D])
    key_rows = split_sequences(projected[:, :, D:2 * D])
    value_rows = split_sequences(projected[:, :, 2 * D:])
    attended = lax.map(jax.checkpoint(attend_one), (queries, key_rows, value_rows, segments.T))
    attended = jnp.transpose(attended, (1, 0, 2, 3)).reshape(LEN, SEQS, D)
    attended = low(low_back(attended))
    branch = jnp.einsum('psd,df->psf', attended, out_weight, precision=HIGHEST) + out_bias
    residual = residual + low_back(branch)
    normed_ff = low(layer_norm(residual, norm2_gain, norm2_shift))
    hidden = jnp.einsum('psd,df->psf', normed_ff, up_weight, precision=HIGHEST) + up_bias
    hidden = low_back(hidden)
    activated = low(jax.nn.gelu(hidden, approximate=False))
    branch = jnp.einsum('psf,fd->psd', activated, down_weight, precision=HIGHEST) + down_bias
    return residual + low_back(branch)

def stack_forward(start_rows, segments, params):
    residual = start_rows
    for layer_index in range(LAYERS):
        residual = block_layer(residual, segments, [tensor[layer_index] for tensor in params])
    return residual

def reference(tokens, segments, cotangent, norm1_gain, norm1_shift, qkv_weight, qv_bias, out_weight, out_bias, norm2_gain, norm2_shift, up_weight, up_bias, down_weight, down_bias):
    params = [argument.astype(jnp.float32) for argument in (norm1_gain, norm1_shift, qkv_weight, qv_bias, out_weight, out_bias, norm2_gain, norm2_shift, up_weight, up_bias, down_weight, down_bias)]

    def closed(start_rows, *weights):
        return stack_forward(start_rows, segments, weights)
    output, pullback = jax.vjp(closed, tokens.astype(jnp.float32), *params)
    gradients = pullback(cotangent.astype(jnp.float32))
    return (output.astype(jnp.bfloat16), gradients[0], gradients[1], gradients[2], gradients[3], gradients[4], gradients[5], gradients[6], gradients[7], gradients[8], gradients[9], gradients[10], gradients[11], gradients[12])
```

```python
import functools

import jax
import jax.numpy as jnp
from jax import lax
from jax.experimental import pallas as pl
from jax.experimental.pallas import tpu as pltpu
from jax.sharding import PartitionSpec as P

D = 1088
HEADS = 17
HEAD = 64
FF = 4352
LAYERS = 2

EPSILON = 1e-05
NEGATIVE = -1e30
SCORE_SCALE = 0.125
BF = jnp.bfloat16
F32 = jnp.float32
MESH = pl.DeviceIdType.MESH
ANY = pl.BlockSpec(memory_space=pl.ANY)
VMEM = pl.BlockSpec(memory_space=pltpu.VMEM)
VMEM_LIMIT = 58 << 20


class Dims:
    def __init__(self, mesh, length):
        self.dp, self.wide, self.narrow = (mesh.shape[a] for a in ("dp", "wide", "narrow"))
        assert self.narrow == 2 and self.wide & (self.wide - 1) == 0
        self.block = length // (self.wide * self.narrow)
        self.pos = self.wide * self.block
        self.half = D // self.narrow
        self.ff = FF // self.wide
        self.qc = 3 * D // self.wide
        self.oc = D // self.wide
        base, extra = divmod(HEADS, self.wide)
        self.base, self.extra = base, extra
        self.starts = [t * base + min(t, extra) for t in range(self.wide + 1)]
        self.slots = base + (extra > 0)
        self.hq = self.slots * HEAD
        self.peers = sorted(range(1, self.wide), key=lambda k: -bin(k).count("1"))

    def pieces(self, kinds, src_rows):
        found = []
        for t in range(self.wide):
            for y in range(kinds):
                low = y * D + self.starts[t] * HEAD
                high = y * D + self.starts[t + 1] * HEAD
                for s in range(self.wide):
                    a, b = max(low, s * src_rows), min(high, (s + 1) * src_rows)
                    if a < b:
                        found.append((s, t, a - s * src_rows, y * self.hq + a - low, b - a))
        return found

    def gaps(self, kinds):
        return [
            (t, y * self.hq + (self.starts[t + 1] - self.starts[t]) * HEAD)
            for t in range(self.wide)
            if self.starts[t + 1] - self.starts[t] < self.slots
            for y in range(kinds)
        ]


def flip(number, bits):
    for bit in (1, 2, 4, 8, 16):
        if bits & bit:
            number = number + bit - 2 * bit * ((number // bit) % 2)
    return number


class Place:
    def __init__(self, dm):
        self.dm = dm
        self.z, self.w, self.n = (lax.axis_index(a) for a in ("dp", "wide", "narrow"))

    def core(self):
        return (self.z, self.w, 1 - self.n)

    def chip(self, k):
        return (self.z, flip(self.w, k), self.n)

    def chip_at(self, t):
        return (self.z, t, self.n)

    def lanes(self, k):
        b = self.dm.block
        return pl.ds(pl.multiple_of(flip(self.w, k) * b, b), b)

    def half(self, n):
        h = self.dm.half
        return pl.ds(pl.multiple_of(n * h, 16), h)

    def barrier(self):
        sem = pltpu.get_barrier_semaphore()
        for k in self.dm.peers:
            pl.semaphore_signal(sem, inc=1, device_id=self.chip(k), device_id_type=MESH)
        pl.semaphore_signal(sem, inc=1, device_id=self.core(), device_id_type=MESH)
        pl.semaphore_wait(sem, len(self.dm.peers) + 1)


def remote(src, dst, send, recv, device):
    return pltpu.make_async_remote_copy(
        src_ref=src, dst_ref=dst, send_sem=send, recv_sem=recv, device_id=device, device_id_type=MESH
    )


class Local:
    def __init__(self, sems):
        self.sems, self.used, self.all = sems, 0, []

    def start(self, src, dst):
        copy = pltpu.make_async_copy(src, dst, self.sems.at[self.used])
        self.used += 1
        copy.start()
        self.all.append(copy)
        return copy


def loop(total, chunk, body):
    def step(i, carry):
        body(pl.ds(pl.multiple_of(i * chunk, 16), chunk))
        return carry

    lax.fori_loop(0, total // chunk, step, 0)


def dot(a, b):
    return jnp.dot(a, b, preferred_element_type=F32)


def dot_nt(a, b):
    return lax.dot_general(a, b, (((1,), (1,)), ((), ())), preferred_element_type=F32)


def dot_tn(a, b):
    return lax.dot_general(a, b, (((0,), (0,)), ((), ())), preferred_element_type=F32)


class Exchange:
    def __init__(self, at, send, recv):
        self.at, self.send, self.recv = at, send, recv

    def gather_start(self, buf):
        at = self.at
        own = buf.at[:, at.lanes(0)]
        for k in at.dm.peers:
            remote(own, own, self.send.at[k - 1], self.recv.at[k - 1], at.chip(k)).start()

    def gather_wait(self, buf):
        at = self.at
        own = buf.at[:, at.lanes(0)]
        for k in at.dm.peers:
            there = buf.at[:, at.lanes(k)]
            remote(own, there, self.send.at[k - 1], self.recv.at[k - 1], at.chip(k)).wait()

    def project(self, weight, source, sbuf, rbuf, own):
        at = self.at
        for k in at.dm.peers + [0]:
            block = source[:, at.lanes(k)]

            def part(r, k=k, block=block):
                term = dot(weight[r, :], block)
                if k:
                    sbuf[k - 1, r, :] = term.astype(BF)
                else:
                    own[r, :] = term

            loop(D, D // 4, part)
            if k:
                self.copy(sbuf, rbuf, k).start()

    def copy(self, sbuf, rbuf, k):
        return remote(
            sbuf.at[k - 1], rbuf.at[k - 1], self.send.at[k - 1], self.recv.at[k - 1], self.at.chip(k)
        )

    def total(self, sbuf, rbuf, own):
        for k in self.at.dm.peers:
            self.copy(sbuf, rbuf, k).wait()
        value = own[...]
        for k in self.at.dm.peers:
            value = value + rbuf[k - 1].astype(F32)
        return value


def norm_stats(x):
    mean = jnp.sum(x, 0, keepdims=True) / D
    centered = x - mean
    variance = jnp.sum(centered * centered, 0, keepdims=True) / D
    return centered, lax.rsqrt(variance + EPSILON)


def norm_forward(x, gain, shift):
    centered, inv = norm_stats(x)
    return centered * inv * gain + shift


def norm_backward(q, x, gain):
    centered, inv = norm_stats(x)
    n = centered * inv
    e = q * gain
    grad = inv * (
        e - jnp.sum(e, 0, keepdims=True) / D - n * (jnp.sum(e * n, 0, keepdims=True) / D)
    )
    return grad, jnp.sum(q * n, 1, keepdims=True), jnp.sum(q, 1, keepdims=True)


def gelu_parts(h):
    cdf = 0.5 * (1.0 + lax.erf(h * 0.7071067811865476))
    return cdf, h * cdf


def mask_bias(dm, segk, segq, n, bias):
    shape = (dm.pos, dm.pos)
    ki = lax.broadcasted_iota(jnp.int32, shape, 0)
    qi = lax.broadcasted_iota(jnp.int32, shape, 1)
    qpos = (qi // dm.block) * (2 * dm.block) + n * dm.block + qi % dm.block
    for c in range(2):
        kpos = (ki // dm.block) * (2 * dm.block) + c * dm.block + ki % dm.block
        same = segk[c * dm.pos : (c + 1) * dm.pos, :] == segq[...]
        bias[c] = jnp.where(same & (kpos <= qpos), 0.0, NEGATIVE)


def chunk_list(dm):
    step = dm.pos // 2
    return [(slice(0, step), step), (slice(step, 2 * step), 2 * step)]


def prep_kernel(
    dm, wq_in, wo_in, wu_in, wd_in, tok, cot,
    wq, wo, wu, wd, x0, ct,
    zero, lsem, psend, precv, csend, crecv,
):
    at = Place(dm)
    n, w = at.n, at.w
    at.barrier()
    zero[...] = jnp.zeros_like(zero)
    plan_q, plan_o = dm.pieces(3, dm.qc), dm.pieces(1, dm.oc)
    local, far, swap = [], [], []
    for l in range(LAYERS):
        for plan, src, dst in ((plan_q, wq_in, wq), (plan_o, wo_in, wo)):
            for s, t, a, b, rows in plan:
                here, there = src.at[l, pl.ds(a, rows)], dst.at[l, n, pl.ds(b, rows)]
                if s == t:
                    local.append((w == s, here, there))
                else:
                    far.append((s, t, here, there))
        for kinds, dst in ((3, wq), (1, wo)):
            for t, row in dm.gaps(kinds):
                local.append((w == t, zero, dst.at[l, n, pl.ds(row, HEAD)]))
        for src, dst in ((wu_in, wu), (wd_in, wd)):
            there = dst.at[l, at.half(n)]
            local.append((None, src.at[l], there))
            swap.append((src.at[l], there))
    for src, dst in ((tok, x0), (cot, ct)):
        b = dm.block
        mine = src.at[:, pl.ds(pl.multiple_of(n * b, b), b)]
        other = src.at[:, pl.ds(pl.multiple_of((1 - n) * b, b), b)]
        there = dst.at[at.half(n)]
        local.append((None, mine, there))
        swap.append((other, there))

    def far_copy(i):
        s, t, here, there = far[i]
        return remote(here, there, psend.at[i], precv.at[i], at.chip_at(t))

    def local_copy(i):
        return pltpu.make_async_copy(local[i][1], local[i][2], lsem.at[i])

    def swap_copy(i):
        here, there = swap[i]
        return remote(here, there, csend.at[i], crecv.at[i], at.core())

    def when(cond, fn):
        if cond is None:
            fn()
        else:
            pl.when(cond)(fn)

    for i in range(len(far)):
        when(w == far[i][0], lambda i=i: far_copy(i).start())
    for i in range(len(local)):
        when(local[i][0], lambda i=i: local_copy(i).start())
    for i in range(len(swap)):
        swap_copy(i).start()
    for i in range(len(far)):
        when(w == far[i][1], lambda i=i: far_copy(i).wait_recv())
    for i in range(len(local)):
        when(local[i][0], lambda i=i: local_copy(i).wait())
    first = len(swap)
    for l in range(LAYERS):
        swap.append((wq.at[l, n], wq.at[l, n]))
        swap.append((wo.at[l, n], wo.at[l, n]))
    for i in range(first, len(swap)):
        swap_copy(i).start()
    for i in range(len(far)):
        when(w == far[i][0], lambda i=i: far_copy(i).wait_send())
    for i in range(len(swap)):
        swap_copy(i).wait()


def forward_kernel(
    dm, layer, x_in, pk, segk, segq, wq_all, wo_all, wu_all, wd_all,
    x_out, xg1_o, q_o, kv_o, lse_o, att_o, xmid_o, xg2_o, hid_o,
    wq, wo, wu, wd, wqf, wot, wut, xg1, xg2, q, kv, lse, att, xmid, hid, act, bias, cols,
    sbuf, rbuf, own, lsem, ssem, rsem, csem,
):
    at = Place(dm)
    n = at.n
    at.barrier()
    local = Local(lsem)
    loads = [
        local.start(src.at[layer], dst)
        for src, dst in ((wq_all, wq), (wo_all, wo), (wu_all, wu), (wd_all, wd))
    ]
    ex = [Exchange(at, ssem.at[i], rsem.at[i]) for i in range(4)]
    cols[...] = pk[...].T

    def col(i, rows=slice(None)):
        return cols[rows, i : i + 1]

    xg1[:, at.lanes(0)] = norm_forward(x_in[...].astype(F32), col(0), col(1)).astype(BF)
    ex[0].gather_start(xg1)
    mask_bias(dm, segk, segq, n, bias)
    loads[0].wait()
    wqf[...] = jnp.concatenate([wq[0].T, wq[1].T], 0).T
    loads[1].wait()
    wot[: dm.half, :] = wo[0].T
    wot[dm.half :, :] = wo[1].T
    ex[0].gather_wait(xg1)
    saves = [local.start(xg1, xg1_o)]

    def project_q(r):
        term = dot(wqf[r, :], xg1[...]) + col(7, r)
        q[r, :] = (term.astype(BF).astype(F32) * SCORE_SCALE).astype(BF)

    def project_kv(r):
        rows = pl.ds(pl.multiple_of(r.start + dm.hq, 16), r.size)
        kv[n, r, :] = (dot(wqf[rows, :], xg1[...]) + col(7, rows)).astype(BF)

    loop(2 * dm.hq, dm.hq // 2, project_kv)
    swap = remote(kv.at[n], kv.at[n], csem.at[0], csem.at[1], at.core())
    swap.start()
    loop(dm.hq, dm.hq // 2, project_q)
    saves.append(local.start(q, q_o))
    loads[2].wait()
    wut[...] = wu[...].T
    remote(kv.at[n], kv.at[1 - n], csem.at[0], csem.at[1], at.core()).wait()
    saves.append(local.start(kv, kv_o))

    def head(h, carry):
        r = pl.ds(pl.multiple_of(h * HEAD, HEAD), HEAD)
        rv = pl.ds(pl.multiple_of(h * HEAD + dm.hq, HEAD), HEAD)
        for lanes, keys in chunk_list(dm):
            k_all = jnp.concatenate([kv[0, r, :keys], kv[1, r, :keys]], 1)
            v_all = jnp.concatenate([kv[0, rv, :keys], kv[1, rv, :keys]], 1)
            b_all = jnp.concatenate([bias[0, :keys, lanes], bias[1, :keys, lanes]], 0)
            s = dot_tn(k_all, q[r, lanes]) + b_all
            top = jnp.max(s, 0, keepdims=True)
            p = jnp.exp(s - top)
            total = jnp.sum(p, 0, keepdims=True)
            att[r, lanes] = (dot(v_all, p.astype(BF)) / total).astype(BF)
            lse[pl.ds(h, 1), lanes] = top + jnp.log(total)
        return carry

    lax.fori_loop(0, dm.slots, head, 0)
    saves.append(local.start(lse, lse_o))
    saves.append(local.start(att, att_o))
    ex[1].project(wot, att, sbuf.at[0], rbuf.at[0], own)
    branch = ex[1].total(sbuf.at[0], rbuf.at[0], own)
    xmid[...] = x_in[...].astype(F32) + (branch + col(4))
    saves.append(local.start(xmid, xmid_o))
    xg2[:, at.lanes(0)] = norm_forward(xmid[...], col(2), col(3)).astype(BF)
    ex[2].gather_start(xg2)
    loads[3].wait()
    ex[2].gather_wait(xg2)
    saves.append(local.start(xg2, xg2_o))

    def up(r):
        h = dot(wut[r, :], xg2[...]) + col(6, r)
        hid[r, :] = h
        act[r, :] = gelu_parts(h)[1].astype(BF)

    loop(dm.ff, dm.ff // 4, up)
    saves.append(local.start(hid, hid_o))
    ex[3].project(wd, act, sbuf.at[1], rbuf.at[1], own)
    branch = ex[3].total(sbuf.at[1], rbuf.at[1], own)
    x_out[...] = xmid[...] + (branch + col(5))
    for copy in saves:
        copy.wait()


def backward_kernel(
    dm, layer, gx_in, x_in, pk, segk, segq, wq_all, wo_all, wu_all, wd_all,
    xg1_i, q_i, kv_i, lse_i, att_i, xmid_i, xg2_i, hid_i,
    gx_out, gd_o, gu_o, gq_o, go_o, small,
    wq, wo, wu, wdt, wd, wqt, xg1, xg2, q, kv, lse, att, xmid, hid, act, gh, bias, cols, sums,
    gb, gab, gatt, gp, dkv, dsend, drecv, gmid, gacc, gsend, grecv, gq, go,
    gqs, gqr, gos, gor, sbuf, rbuf, own, lsem, ssem, rsem, csend, crecv, psend, precv,
):
    at = Place(dm)
    n, w = at.n, at.w
    at.barrier()
    local = Local(lsem)
    ld = {}
    for name, src, dst in (
        ("hid", hid_i, hid), ("wd", wd_all.at[layer], wdt), ("wu", wu_all.at[layer], wu),
        ("xmid", xmid_i, xmid), ("xg2", xg2_i, xg2),
        ("wo", wo_all.at[layer], wo), ("wq", wq_all.at[layer], wq), ("q", q_i, q), ("kv", kv_i, kv),
        ("lse", lse_i, lse), ("att", att_i, att), ("xg1", xg1_i, xg1),
    ):
        ld[name] = local.start(src, dst)
    ex = [Exchange(at, ssem.at[i], rsem.at[i]) for i in range(4)]
    cols[...] = pk[...].T
    sums[...] = jnp.zeros_like(sums)

    def col(i, rows=slice(None)):
        return cols[rows, i : i + 1]

    def col_sum(value):
        return jnp.sum(value, 1, keepdims=True)

    swaps = []

    def swap_start(src, dst):
        i = len(swaps)
        copy = remote(src, dst, csend.at[i], crecv.at[i], at.core())
        swaps.append(copy)
        copy.start()
        return copy

    g = gx_in[...].astype(BF)
    gb[:, at.lanes(0)] = g
    ex[0].gather_start(gb)
    sums[:, 5:6] = col_sum(g.astype(F32))
    ld["wd"].wait()
    wd[...] = wdt[...].T
    ld["hid"].wait()

    def gelu_both(r):
        h = hid[r, :]
        cdf, value = gelu_parts(h)
        act[r, :] = value.astype(BF)
        hid[r, :] = cdf + h * (jnp.exp(h * h * -0.5) * 0.3989422804014327)

    loop(dm.ff, dm.ff // 4, gelu_both)
    ld["wu"].wait()
    ex[0].gather_wait(gb)

    def grad_hidden(r):
        value = (dot(wd[r, :], gb[...]) * hid[r, :]).astype(BF)
        gh[r, :] = value
        sums[r, 6:7] = col_sum(value.astype(F32))

    loop(dm.ff, dm.ff // 4, grad_hidden)
    ex[1].project(wu, gh, sbuf.at[0], rbuf.at[0], own)

    ld["xg2"].wait()
    for i, (left, right, out) in enumerate(((gb, act, gd_o), (xg2, gh, gu_o))):

        def other_half(r, left=left, right=right, i=i):
            rows = pl.ds(pl.multiple_of((1 - n) * dm.half + r.start, 16), r.size)
            gsend[i, r, :] = dot_nt(left[rows, :], right[...]).astype(BF)

        loop(dm.half, dm.half // 2, other_half)
        swap_start(gsend.at[i], grecv.at[i])

        def own_half(r, left=left, right=right):
            rows = pl.ds(pl.multiple_of(n * dm.half + r.start, 16), r.size)
            gacc[r, :] = dot_nt(left[rows, :], right[...])

        loop(dm.half, dm.half // 2, own_half)
        swaps[i].wait()

        def add(r, i=i, out=out):
            out[r, :] = (gacc[r, :] + grecv[i, r, :].astype(F32)).astype(BF)

        loop(dm.half, dm.half // 2, add)

    ld["xmid"].wait()
    grad_normed = ex[1].total(sbuf.at[0], rbuf.at[0], own)
    grad, grad_gain, grad_shift = norm_backward(grad_normed, xmid[...], col(2))
    sums[:, 2:3] = grad_gain
    sums[:, 3:4] = grad_shift
    value = gx_in[...].astype(F32) + grad
    gmid[...] = value
    g = value.astype(BF)
    gab[:, at.lanes(0)] = g
    ex[2].gather_start(gab)
    sums[:, 4:5] = col_sum(g.astype(F32))
    mask_bias(dm, segk, segq, n, bias)
    for name in ("wq", "wo", "q", "kv", "lse", "att"):
        ld[name].wait()
    wqt[: dm.half, :] = wq[0].T
    wqt[dm.half :, :] = wq[1].T
    ex[2].gather_wait(gab)
    gatt[...] = (dot(wo[0], gab[: dm.half, :]) + dot(wo[1], gab[dm.half :, :])).astype(BF)

    def head(h, carry):
        r = pl.ds(pl.multiple_of(h * HEAD, HEAD), HEAD)
        rv = pl.ds(pl.multiple_of(h * HEAD + dm.hq, HEAD), HEAD)
        for i, (lanes, keys) in enumerate(chunk_list(dm)):
            k_all = jnp.concatenate([kv[0, r, :keys], kv[1, r, :keys]], 1)
            v_all = jnp.concatenate([kv[0, rv, :keys], kv[1, rv, :keys]], 1)
            b_all = jnp.concatenate([bias[0, :keys, lanes], bias[1, :keys, lanes]], 0)
            qs, go_h = q[r, lanes], gatt[r, lanes]
            s = dot_tn(k_all, qs) + b_all
            p = jnp.exp(s - lse[pl.ds(h, 1), lanes])
            dp = dot_tn(v_all, go_h)
            delta = jnp.sum(p * dp, 0, keepdims=True)
            ds = (p * (dp - delta)).astype(BF)
            gp[r, lanes] = (dot(k_all, ds) * SCORE_SCALE).astype(BF)
            dk = dot_nt(qs, ds)
            dv = dot_nt(go_h, p.astype(BF))
            for c in range(2):
                part = slice(c * keys, (c + 1) * keys)
                if i == 0:
                    dkv[c, r, :keys] = dk[:, part]
                    dkv[c, rv, :keys] = dv[:, part]
                    dkv[c, r, keys:] = jnp.zeros((HEAD, dm.pos - keys), F32)
                    dkv[c, rv, keys:] = jnp.zeros((HEAD, dm.pos - keys), F32)
                else:
                    dkv[c, r, :] += dk[:, part]
                    dkv[c, rv, :] += dv[:, part]
        return carry

    lax.fori_loop(0, dm.slots, head, 0)
    dsend[...] = dkv[1 - n].astype(BF)
    swap_start(dsend, drecv).wait()

    def join(r):
        rows = pl.ds(pl.multiple_of(r.start + dm.hq, 16), r.size)
        gp[rows, :] = (dkv[n, r, :] + drecv[r, :].astype(F32)).astype(BF)

    loop(2 * dm.hq, dm.hq // 2, join)

    def bias_sum(r):
        sums[r, 7:8] = col_sum(gp[r, :].astype(F32))

    loop(3 * dm.hq, dm.hq // 2, bias_sum)
    ex[3].project(wqt, gp, sbuf.at[1], rbuf.at[1], own)

    ld["xg1"].wait()
    gos[...] = dot_nt(att[...], gab[at.half(1 - n), :]).astype(BF)
    swap_o = swap_start(gos, gor)

    def gq_other(r):
        gqs[r, :] = dot_nt(gp[r, :], xg1[at.half(1 - n), :]).astype(BF)

    loop(3 * dm.hq, dm.hq // 2, gq_other)
    swap_q = swap_start(gqs, gqr)
    go_own = dot_nt(att[...], gab[at.half(n), :])
    swap_o.wait()
    go[...] = (go_own + gor[...].astype(F32)).astype(BF)

    def gq_own(r):
        gacc[r, : dm.half] = dot_nt(gp[r, :], xg1[at.half(n), :])

    loop(3 * dm.hq, dm.hq // 2, gq_own)
    swap_q.wait()

    def gq_add(r):
        gq[r, :] = (gacc[r, : dm.half] + gqr[r, :].astype(F32)).astype(BF)

    loop(3 * dm.hq, dm.hq // 2, gq_add)

    far, here = [], []
    for plan, src, dst in (
        (dm.pieces(3, dm.qc), gq, gq_o), (dm.pieces(1, dm.oc), go, go_o),
    ):
        for s, t, a, b, rows in plan:
            entry = (s, t, src.at[pl.ds(b, rows)], dst.at[pl.ds(a, rows)])
            (here if s == t else far).append(entry)

    def far_copy(i):
        s, t, source, target = far[i]
        return remote(source, target, psend.at[i], precv.at[i], at.chip_at(s))

    def here_copy(i):
        s, t, source, target = here[i]
        return pltpu.make_async_copy(source, target, lsem.at[local.used + i])

    for i in range(len(far)):
        pl.when(w == far[i][1])(lambda i=i: far_copy(i).start())
    for i in range(len(here)):
        pl.when(w == here[i][0])(lambda i=i: here_copy(i).start())

    grad_normed = ex[3].total(sbuf.at[1], rbuf.at[1], own)
    grad, grad_gain, grad_shift = norm_backward(grad_normed, x_in[...].astype(F32), col(0))
    sums[:, 0:1] = grad_gain
    sums[:, 1:2] = grad_shift
    gx_out[...] = gmid[...] + grad
    small[...] = sums[...].T
    for i in range(len(far)):
        pl.when(w == far[i][0])(lambda i=i: far_copy(i).wait_recv())
        pl.when(w == far[i][1])(lambda i=i: far_copy(i).wait_send())
    for i in range(len(here)):
        pl.when(w == here[i][0])(lambda i=i: here_copy(i).wait())


def struct(*shape, dtype=BF):
    return jax.ShapeDtypeStruct(shape, dtype)


def call(kernel, ident, outs, in_specs, out_specs, scratch):
    return pl.pallas_call(
        kernel,
        out_shape=outs,
        in_specs=in_specs,
        out_specs=out_specs,
        scratch_shapes=scratch,
        compiler_params=pltpu.CompilerParams(
            collective_id=ident, has_side_effects=True, vmem_limit_bytes=VMEM_LIMIT
        ),
    )


def dma(*shape):
    return pltpu.SemaphoreType.DMA(shape)


def prepare(dm, wq, wo, wu, wd, tok, cot):
    far = sum(s != t for s, t, *_ in dm.pieces(3, dm.qc) + dm.pieces(1, dm.oc)) * LAYERS
    near = (
        sum(s == t for s, t, *_ in dm.pieces(3, dm.qc) + dm.pieces(1, dm.oc))
        + len(dm.gaps(4)) + 2
    ) * LAYERS + 2
    swaps = LAYERS * 4 + 2
    return call(
        functools.partial(prep_kernel, dm),
        0,
        [
            struct(LAYERS, 2, 3 * dm.hq, dm.half), struct(LAYERS, 2, dm.hq, dm.half),
            struct(LAYERS, D, dm.ff), struct(LAYERS, D, dm.ff),
            struct(D, dm.block), struct(D, dm.block),
        ],
        [ANY] * 6,
        [ANY] * 6,
        [pltpu.VMEM((HEAD, dm.half), BF), dma(near), dma(far), dma(far), dma(swaps), dma(swaps)],
    )(wq, wo, wu, wd, tok, cot)


def saved_shapes(dm):
    return [
        struct(D, dm.pos), struct(dm.hq, dm.pos), struct(2, 2 * dm.hq, dm.pos),
        struct(8, dm.pos, dtype=F32), struct(dm.hq, dm.pos), struct(D, dm.block, dtype=F32),
        struct(D, dm.pos), struct(dm.ff, dm.pos, dtype=F32),
    ]


def forward(dm, layer, x, pk, segk, segq, weights):
    v, steps = pltpu.VMEM, len(dm.peers)
    return call(
        functools.partial(forward_kernel, dm, layer),
        1 + layer,
        [struct(D, dm.block, dtype=F32)] + saved_shapes(dm),
        [VMEM] * 4 + [ANY] * 4,
        [VMEM] + [ANY] * 8,
        [
            v((2, 3 * dm.hq, dm.half), BF), v((2, dm.hq, dm.half), BF), v((D, dm.ff), BF),
            v((D, dm.ff), BF), v((3 * dm.hq, D), BF), v((D, dm.hq), BF), v((dm.ff, D), BF),
            v((D, dm.pos), BF), v((D, dm.pos), BF), v((dm.hq, dm.pos), BF),
            v((2, 2 * dm.hq, dm.pos), BF), v((8, dm.pos), F32), v((dm.hq, dm.pos), BF),
            v((D, dm.block), F32), v((dm.ff, dm.pos), F32), v((dm.ff, dm.pos), BF),
            v((2, dm.pos, dm.pos), F32), v((D, 8), F32),
            v((2, steps, D, dm.block), BF), v((2, steps, D, dm.block), BF), v((D, dm.block), F32),
            dma(16), dma(4, steps), dma(4, steps), dma(2),
        ],
    )(x, pk, segk, segq, *weights)


def backward(dm, layer, gx, x, pk, segk, segq, weights, saved):
    v, steps = pltpu.VMEM, len(dm.peers)
    far = sum(s != t for s, t, *_ in dm.pieces(3, dm.qc) + dm.pieces(1, dm.oc))
    return call(
        functools.partial(backward_kernel, dm, layer),
        8 + layer,
        [
            struct(D, dm.block, dtype=F32), struct(dm.half, dm.ff), struct(dm.half, dm.ff),
            struct(dm.qc, dm.half), struct(dm.oc, dm.half), struct(8, D, dtype=F32),
        ],
        [VMEM] * 5 + [ANY] * 12,
        [VMEM] * 3 + [ANY] * 2 + [VMEM],
        [
            v((2, 3 * dm.hq, dm.half), BF), v((2, dm.hq, dm.half), BF), v((D, dm.ff), BF),
            v((D, dm.ff), BF), v((dm.ff, D), BF), v((D, 3 * dm.hq), BF),
            v((D, dm.pos), BF), v((D, dm.pos), BF), v((dm.hq, dm.pos), BF),
            v((2, 2 * dm.hq, dm.pos), BF), v((8, dm.pos), F32), v((dm.hq, dm.pos), BF),
            v((D, dm.block), F32), v((dm.ff, dm.pos), F32), v((dm.ff, dm.pos), BF),
            v((dm.ff, dm.pos), BF), v((2, dm.pos, dm.pos), F32), v((D, 8), F32), v((D, 8), F32),
            v((D, dm.pos), BF), v((D, dm.pos), BF), v((dm.hq, dm.pos), BF),
            v((3 * dm.hq, dm.pos), BF), v((2, 2 * dm.hq, dm.pos), F32),
            v((2 * dm.hq, dm.pos), BF), v((2 * dm.hq, dm.pos), BF), v((D, dm.block), F32),
            v((D, dm.ff), F32), v((2, dm.half, dm.ff), BF), v((2, dm.half, dm.ff), BF),
            v((3 * dm.hq, dm.half), BF), v((dm.hq, dm.half), BF),
            v((3 * dm.hq, dm.half), BF), v((3 * dm.hq, dm.half), BF),
            v((dm.hq, dm.half), BF), v((dm.hq, dm.half), BF),
            v((2, steps, D, dm.block), BF), v((2, steps, D, dm.block), BF), v((D, dm.block), F32),
            dma(32), dma(4, steps), dma(4, steps), dma(5), dma(5), dma(far), dma(far),
        ],
    )(gx, x, pk, segk, segq, *weights, *saved)


def swap_halves(values, half):
    n = lax.axis_index("narrow")
    parts = values.reshape(2, half, values.shape[1])
    return lax.all_to_all(parts, "narrow", split_axis=0, concat_axis=2, tiled=True)[0]


def per_device(
    dm, tokens, segments, cotangent, norm1_gain, norm1_shift, qkv_weight, qv_bias, out_weight,
    out_bias, norm2_gain, norm2_shift, up_weight, up_bias, down_weight, down_bias,
):
    w, n = lax.axis_index("wide"), lax.axis_index("narrow")
    wq = jnp.swapaxes(qkv_weight, 1, 2)
    wd = jnp.swapaxes(down_weight, 1, 2)
    tok, cot = tokens[:, 0, :].T, cotangent[:, 0, :].T
    *weights, x0, ct = prepare(dm, wq, out_weight, up_weight, wd, tok, cot)

    head_row = (w * dm.base + jnp.minimum(w, dm.extra)) * HEAD

    def head_part(vector):
        padded = jnp.pad(vector, ((0, 0), (0, HEAD)))
        return lax.dynamic_slice_in_dim(padded, head_row, dm.hq, 1)

    qkv_bias = jnp.concatenate(
        [
            head_part(qv_bias[:, 0]), jnp.zeros((LAYERS, dm.hq), F32), head_part(qv_bias[:, 1]),
            jnp.zeros((LAYERS, D - 3 * dm.hq), F32),
        ],
        1,
    )
    up_part = lax.dynamic_slice_in_dim(up_bias, w * dm.ff, dm.ff, 1)
    pk = jnp.stack(
        [norm1_gain, norm1_shift, norm2_gain, norm2_shift, out_bias, down_bias, up_part, qkv_bias],
        1,
    )
    seg = segments[:, 0].reshape(dm.wide, 2, dm.block).transpose(1, 0, 2).reshape(2, dm.pos)
    segk = seg.reshape(2 * dm.pos, 1)
    segq = lax.dynamic_slice_in_dim(seg, n, 1, 0)

    x, stored = x0, []
    for layer in range(LAYERS):
        x_next, *saved = forward(dm, layer, x, pk[layer], segk, segq, weights)
        stored.append((x, saved))
        x = x_next
    output = swap_halves(x.astype(BF), dm.half).T[:, None, :]
    gx, grads = ct, [None] * LAYERS
    for layer in reversed(range(LAYERS)):
        x, saved = stored[layer]
        gx, *grads[layer] = backward(dm, layer, gx, x, pk[layer], segk, segq, weights, saved)
    input_grad = swap_halves(gx, dm.half).T[:, None, :]

    def summed(i, turned):
        value = jnp.stack([grads[layer][i] for layer in range(LAYERS)])
        value = lax.psum(value, "dp").astype(F32)
        return jnp.swapaxes(value, 1, 2) if turned else value

    small = jnp.stack([grads[layer][4] for layer in range(LAYERS)])

    def placed(values, start, total):
        return lax.dynamic_update_slice_in_dim(
            jnp.zeros((LAYERS, total), F32), values, start, 1
        )

    q_sum = placed(small[:, 7, : dm.hq], head_row, D + HEAD)
    v_sum = placed(small[:, 7, 2 * dm.hq : 3 * dm.hq], head_row, D + HEAD)
    u_sum = placed(small[:, 6, : dm.ff], w * dm.ff, FF)
    small, q_sum, v_sum, u_sum = lax.psum(
        (small[:, :6], q_sum, v_sum, u_sum), ("dp", "wide", "narrow")
    )
    return (
        output,
        input_grad,
        small[:, 0],
        small[:, 1],
        summed(2, True),
        jnp.stack([q_sum[:, :D], v_sum[:, :D]], 1),
        summed(3, False),
        small[:, 4],
        small[:, 2],
        small[:, 3],
        summed(1, False),
        u_sum,
        summed(0, True),
        small[:, 5],
    )


def solution(mesh):
    def local(tokens, segments, *rest):
        return per_device(Dims(mesh, segments.shape[0]), tokens, segments, *rest)

    rows = P("wide", "dp", "narrow")
    column, row = P(None, "narrow", "wide"), P(None, "wide", "narrow")
    return jax.shard_map(
        local,
        mesh=mesh,
        in_specs=(
            rows, P(None, "dp"), rows, P(), P(), column, P(), row, P(), P(), P(), column, P(), row, P(),
        ),
        out_specs=(
            rows, rows, P(), P(), column, P(), row, P(), P(), P(), column, P(), row, P(),
        ),
        check_vma=False,
    )
```
